512 devices in a mesh: ctx: 64 (over z_lo, y, core), ch: 8 (over z_hi, x).
Axes of the slice: x: 4, y: 8, z: 8 (z_hi: 2, z_lo: 4; z = z_hi * 4 + z_lo), core: 2. Of those that a mesh axis runs over, the one named last changes fastest.
Arguments:
- projections: bfloat16 [3, 8192, 8192], P(None, 'ctx', 'ch'), may hold values from -150 to 150
- grouped_short_filters: float32 [3, 7, 512], P(None, None, 'ch'), may hold values from -2 to 2
- long_filter: float32 [8192, 8192], P('ctx', 'ch'), may hold values from 0 to 0.5
- norm_gain: float32 [8192], P('ch'), may hold values from 0.1 to 1.9
- out_grad: bfloat16 [8192, 8192], P('ctx', 'ch'), may hold values from -6 to 6
Outputs:
- output: bfloat16 [8192, 8192], P('ctx', 'ch')
- proj_grads: bfloat16 [3, 8192, 8192], P(None, 'ctx', 'ch')
- short_grads: float32 [3, 7, 512], P(None, None, 'ch')
- long_grad: float32 [8192, 8192], P('ctx', 'ch')
- gain_grad: float32 [8192], P('ch')
The draws below stay inside these ranges and needn't reach their ends.
All inputs are finite; a program needn't handle non-finite values.
Results may differ from the reference program's by a relative error of at most 0.0064.
Values may be sent and summed in bfloat16 or wider, within the bound.
A program may use at most 64 MiB of HBM per device.

```python
import math
import jax
import jax.numpy as jnp
from jax import lax

D = 8192
GROUP = 16
KS = 7
TOTAL_TOKENS = 8192
FILTERS = 512


def draw_projections(key, part):
    key_base = jax.random.fold_in(key, 11)
    key_scale = jax.random.fold_in(key, 12)
    chan_pos = jnp.arange(D, dtype=jnp.float32) / D
    chan_scale = jnp.exp(jax.random.uniform(key_scale, (D,), jnp.float32, 0.0, math.log(10.0)))
    chan_scale = chan_scale * jnp.exp(math.log(3.0) * chan_pos)
    base = jnp.clip(jax.random.normal(key_base, (3, TOTAL_TOKENS, D), jnp.float32), -4.0, 4.0)
    ones_row = jnp.ones((D,), jnp.float32)
    factor = jnp.stack([ones_row, ones_row, chan_scale])[:, None, :]
    return (base * factor).astype(jnp.bfloat16)


def draw_long_filter(key, part):
    key_slow = jax.random.fold_in(key, 21)
    key_fast = jax.random.fold_in(key, 22)
    key_pick = jax.random.fold_in(key, 23)
    key_noise = jax.random.fold_in(key, 24)
    spike_seed_state = jax.random.fold_in(key, 25)
    fast_share = 0.5
    slow_tau = jnp.exp(jax.random.uniform(key_slow, (D,), jnp.float32, math.log(TOTAL_TOKENS), math.log(8.0 * TOTAL_TOKENS)))
    fast_tau = jnp.exp(jax.random.uniform(key_fast, (D,), jnp.float32, math.log(12.0), math.log(20.0)))
    is_fast = jax.random.bernoulli(key_pick, fast_share, (D,))
    decay_len = jnp.where(is_fast, fast_tau, slow_tau)
    amplitude = 1.0 / jnp.sqrt(jnp.minimum(decay_len, float(TOTAL_TOKENS)))
    shift_count = jnp.arange(TOTAL_TOKENS, dtype=jnp.int32)
    decay = jnp.exp(-shift_count.astype(jnp.float32)[:, None] / decay_len[None, :])
    spike_offset_index = jax.random.randint(spike_seed_state, (4,), 1, TOTAL_TOKENS)
    masked_elements = jnp.prod(jnp.where(shift_count[:, None] >= spike_offset_index[None, :], 0.65, 1.0), axis=1)
    noise = jax.random.uniform(key_noise, (TOTAL_TOKENS, D), jnp.float32, 0.5, 1.5)
    return (amplitude[None, :] * decay * masked_elements[:, None] * noise).astype(jnp.float32)


def steps_of(own_key, extent, pieces, low, high):
    def one(position, shards_of):
        steps = jax.random.uniform(jax.random.fold_in(jax.random.fold_in(own_key, 6), position), (shards_of,), jnp.float32, low / len(pieces), high / len(pieces))
        return jnp.repeat(jnp.exp(steps), extent[position] // shards_of).reshape((-1,) + (1,) * (len(extent) - position - 1))

    factor_of = one(*pieces[0])
    for cut in pieces[1:]:
        factor_of = factor_of * one(*cut)
    return factor_of


def normal_values(rng, extent, scale, reach, cuts=(), held_as=jnp.bfloat16):
    entries = scale * jax.random.normal(rng, extent, jnp.float32)
    if cuts:
        entries = entries * steps_of(rng, extent, cuts, -0.22, 0.18)
    return jnp.clip(entries, -reach, reach).astype(held_as)


def setup_inputs(seed: int = 0) -> dict:
    key_list = jax.random.split(jax.random.key(seed), 6)
    projections = draw_projections(jax.random.fold_in(key_list[5], 71), 0)
    grouped_short_filters = normal_values(key_list[1], (3, KS, FILTERS), 0.4, 2.0, ((2, 8),), jnp.float32)
    long_filter = draw_long_filter(jax.random.fold_in(key_list[5], 71), 0)
    norm_gain = jnp.clip(1.0 + 0.18 * jax.random.normal(key_list[3], (D,), jnp.float32), 0.1, 1.9)
    out_grad = normal_values(key_list[4], (TOTAL_TOKENS, D), 1.0, 6.0, ((0, 64), (1, 8)))
    return dict(projections=projections, grouped_short_filters=grouped_short_filters, long_filter=long_filter, norm_gain=norm_gain, out_grad=out_grad)


epsilon = 1e-05
channel_block = 256

def causal_short(signal, filters):
    per_chan = jnp.repeat(filters, GROUP, axis=1)
    padded = jnp.pad(signal, ((KS - 1, 0), (0, 0)))
    length = signal.shape[0]
    conv_sum = jnp.zeros(signal.shape, signal.dtype)
    for tap_idx in range(KS):
        conv_sum = conv_sum + per_chan[tap_idx][None, :] * padded[KS - 1 - tap_idx:KS - 1 - tap_idx + length]
    return (conv_sum, padded)

def block_parts(projections, grouped_short_filters, long_filter, offset):
    length = projections.shape[1]
    period = 2 * length
    features = []
    paddings = []
    for proj_idx in range(3):
        signal = lax.dynamic_slice_in_dim(projections[proj_idx], offset, channel_block, 1).astype(jnp.float32)
        filters = lax.dynamic_slice_in_dim(grouped_short_filters[proj_idx], offset // GROUP, channel_block // GROUP, 1)
        conv_sum, padded = causal_short(signal, filters)
        rounded = lax.optimization_barrier(conv_sum.astype(jnp.bfloat16))
        features.append(rounded.astype(jnp.float32))
        paddings.append(padded)
    filter_cols = lax.dynamic_slice_in_dim(long_filter, offset, channel_block, 1)
    mixed_in = features[1] * features[2]
    spec_u = jnp.fft.rfft(mixed_in, n=period, axis=0)
    spec_h = jnp.fft.rfft(filter_cols, n=period, axis=0)
    conv_out = jnp.fft.irfft(spec_u * spec_h, n=period, axis=0)[:length]
    return (features, paddings, spec_u, spec_h, conv_out)

def reference(projections, grouped_short_filters, long_filter, norm_gain, out_grad):
    length = projections.shape[1]
    width = projections.shape[2]
    period = 2 * length
    starts = jnp.arange(width // channel_block, dtype=jnp.int32) * channel_block

    def forward_block(offset):
        features, paddings, spec_u, spec_h, conv_out = block_parts(projections, grouped_short_filters, long_filter, offset)
        return features[0] * conv_out
    gated_out = lax.map(forward_block, starts)
    gated_out = jnp.transpose(gated_out, (1, 0, 2)).reshape(length, width)
    rscale = lax.rsqrt(lax.optimization_barrier(jnp.mean(gated_out * gated_out, axis=1)) + epsilon)
    normed = gated_out * rscale[:, None]
    output = (normed * norm_gain).astype(jnp.bfloat16)
    gradient_float = out_grad.astype(jnp.float32)
    scaled = gradient_float * norm_gain
    inner_total = lax.optimization_barrier(jnp.mean(scaled * normed, axis=1))
    grad_gated = rscale[:, None] * (scaled - normed * inner_total[:, None])
    gain_grad = lax.optimization_barrier(jnp.sum(gradient_float * normed, axis=0))

    def backward_block(offset):
        features, paddings, spec_u, spec_h, conv_out = block_parts(projections, grouped_short_filters, long_filter, offset)
        grad_cols = lax.dynamic_slice_in_dim(grad_gated, offset, channel_block, 1)
        grad_conv = grad_cols * features[0]
        grad_gate = grad_cols * conv_out
        spec_d = jnp.fft.rfft(grad_conv, n=period, axis=0)
        grad_mix = jnp.fft.irfft(jnp.conj(spec_h) * spec_d, n=period, axis=0)[:length]
        long_cols = jnp.fft.irfft(jnp.conj(spec_u) * spec_d, n=period, axis=0)[:length]
        grad_feats = [grad_gate, grad_mix * features[2], grad_mix * features[1]]
        proj_cols = []
        filter_cols = []
        for proj_idx in range(3):
            filters = lax.dynamic_slice_in_dim(grouped_short_filters[proj_idx], offset // GROUP, channel_block // GROUP, 1)
            per_chan = jnp.repeat(filters, GROUP, axis=1)
            cotangent_widened = jnp.pad(grad_feats[proj_idx], ((0, KS - 1), (0, 0)))
            grad_in = jnp.zeros(grad_feats[proj_idx].shape, grad_feats[proj_idx].dtype)
            tap_terms = []
            for tap_idx in range(KS):
                grad_in = grad_in + per_chan[tap_idx][None, :] * cotangent_widened[tap_idx:tap_idx + length]
                shifted = paddings[proj_idx][KS - 1 - tap_idx:KS - 1 - tap_idx + length]
                tap_prod = lax.optimization_barrier(jnp.sum(grad_feats[proj_idx] * shifted, axis=0))
                tap_terms.append(lax.optimization_barrier(jnp.sum(tap_prod.reshape(channel_block // GROUP, GROUP), axis=1)))
            proj_cols.append(grad_in.astype(jnp.bfloat16))
            filter_cols.append(jnp.stack(tap_terms))
        return (jnp.stack(proj_cols), jnp.stack(filter_cols), long_cols)
    proj_blocks, filter_blocks, long_blocks = lax.map(backward_block, starts)
    proj_grads = jnp.transpose(proj_blocks, (1, 2, 0, 3)).reshape(3, length, width)
    short_grads = jnp.transpose(filter_blocks, (1, 2, 0, 3)).reshape(3, KS, width // GROUP)
    long_grad = jnp.transpose(long_blocks, (1, 0, 2)).reshape(length, width)
    return (output, proj_grads, short_grads, long_grad, gain_grad)
```

```python
import functools
import math

import jax
import jax.numpy as jnp
import numpy as np
from jax import lax
from jax.experimental import pallas as pl
from jax.experimental.pallas import tpu as pltpu
from jax.sharding import PartitionSpec as P

D = 8192
GROUP = 16
KS = 7
EPS = 1e-05
MESH = pl.DeviceIdType.MESH
F32 = jnp.float32
BF16 = jnp.bfloat16

NT = 128
NC = 1024
NP = 64
NH = 8
CH = NC // NP
NB = NC // 128
NG = NC // GROUP

X_H, X_U, X_Z, X_D, X_DU, X_DH = range(6)


def split_np(a):
    hi = a.astype(jnp.bfloat16)
    lo = (a - hi.astype(np.float64)).astype(jnp.bfloat16)
    return hi, lo


@functools.lru_cache(maxsize=None)
def tables():
    n1 = np.arange(NP)[None, :]
    k1 = np.arange(NP)[:, None]
    ang = 2 * math.pi * ((n1 * (4 * k1 + 1)) % (4 * NP)) / (4 * NP)
    wa = np.concatenate([np.cos(ang), -np.sin(ang)], axis=0)
    wah, wal = split_np(wa)
    iah, ial = split_np(wa.T / (NP * NT))
    n2 = np.arange(NT)[None, :]
    tw = 2 * math.pi * (n2 * (4 * k1 + 1)) / (4 * NP * NT)
    tr = np.cos(tw).astype(np.float32)
    ti = (-np.sin(tw)).astype(np.float32)
    m = np.arange(NT)
    angb = 2 * math.pi * ((m[:, None] * m[None, :]) % NT) / NT
    c, s = np.cos(angb), np.sin(angb)
    mb = np.block([[c, -s], [s, c]])
    mbh, mbl = split_np(mb)
    ibh, ibl = split_np(mb.T)
    return (
        np.concatenate([wah, wal], axis=1),
        np.concatenate([iah, iah, ial], axis=1),
        mbh, mbl, ibh, ibl, tr, ti,
    )


def split(x):
    hi = x.astype(BF16)
    return hi, (x - hi.astype(F32)).astype(BF16)


def dot(a, b):
    return jnp.dot(a, b, preferred_element_type=F32)


def lanes(b):
    return pl.ds(pl.multiple_of(b * 128, 128), 128)


def kernel(
    proj_hbm, gsf, h_hbm, gain, og_hbm, wa_in, ia_in, mbh_in, mbl_in, ibh_in, ibl_in, tr_in, ti_in,
    out, pg, sg, lg, gg,
    pv, hv, ogv, wa, ia, mbh, mbl, ibh, ibl, tr, ti,
    halo, ext, gext, kf, vf, qT, scT, G, pc, taps, sb, rb, F, bh, bl, SH, SU, SD, SP,
    nsb, nrb, ar1, ar1r, ar1s, ar1q, ar2, ar2r, ar2s, ar2q,
    in_sem, xs, xr, hs, hr, ns, nr, as_, ar_,
):
    me = lax.axis_index("ctx")
    mc = lax.axis_index("ch")
    bar = pltpu.get_barrier_semaphore()

    loads = [
        pltpu.make_async_copy(a, b, in_sem.at[k])
        for k, (a, b) in enumerate([
            (h_hbm, hv), (proj_hbm, pv), (og_hbm, ogv), (wa_in, wa), (ia_in, ia), (mbh_in, mbh),
            (mbl_in, mbl), (ibh_in, ibh), (ibl_in, ibl), (tr_in, tr), (ti_in, ti)])
    ]
    for c in loads:
        c.start()

    def greet(i, _):
        pl.semaphore_signal(bar, inc=1, device_id={"ctx": lax.rem(me + i, NP)}, device_id_type=MESH)
        return _

    lax.fori_loop(1, NP, greet, 0)

    def greet_ch(i, _):
        pl.semaphore_signal(bar, inc=1, device_id={"ch": lax.rem(mc + i, NH)}, device_id_type=MESH)
        return _

    lax.fori_loop(1, NH, greet_ch, 0)

    def rows16(i):
        return pl.ds(pl.multiple_of(i * CH, CH), CH)

    def send_to(k, t):
        return pltpu.make_async_remote_copy(
            src_ref=sb.at[k, rows16(t)], dst_ref=rb.at[k, rows16(me)],
            send_sem=xs.at[k], recv_sem=xr.at[k], device_id={"ctx": t}, device_id_type=MESH)

    def exchange(k):
        def one(i, _):
            send_to(k, lax.rem(me + i, NP)).start()
            return _

        lax.fori_loop(1, NP, one, 0)
        pltpu.make_async_copy(sb.at[k, rows16(me)], rb.at[k, rows16(me)], xr.at[k]).start()

    def arrived(k):
        pltpu.make_async_copy(rb.at[k], rb.at[k], xr.at[k]).wait()

    def sent(k):
        part = sb.at[k, pl.ds(0, NC - CH)]
        pltpu.make_async_copy(part, part, xs.at[k]).wait()

    loads[0].wait()

    def h_block(b, _):
        sb[X_H, pl.ds(pl.multiple_of(b * 128, 128), 128), :] = hv[:, lanes(b)].T.astype(BF16)
        return _

    lax.fori_loop(0, NB, h_block, 0)
    loads[1].wait()

    pl.semaphore_wait(bar, NP - 1 + NH - 1)

    nxt = lax.rem(me + 1, NP)
    prv = lax.rem(me + NP - 1, NP)
    halo_copy = pltpu.make_async_remote_copy(
        src_ref=pv.at[:, pl.ds(NT - 16, 16), :], dst_ref=halo, send_sem=hs.at[0], recv_sem=hr.at[0],
        device_id={"ctx": nxt}, device_id_type=MESH)
    halo_copy.start()
    exchange(X_H)

    member = (
        lax.broadcasted_iota(jnp.int32, (NG, NC), 1) // GROUP
        == lax.broadcasted_iota(jnp.int32, (NG, NC), 0)
    ).astype(F32)
    for i in range(3):
        pc[i, pl.ds(0, KS), :] = jnp.dot(
            gsf[i], member, preferred_element_type=F32, precision=lax.Precision.HIGHEST)
        ext[i, pl.ds(8, NT), :] = pv[i].astype(F32)
    loads[2].wait()

    halo_copy.wait()
    first = jnp.where(me == 0, 0.0, 1.0).astype(F32)
    for i in range(3):
        edge = halo[i].astype(F32)
        ext[i, pl.ds(0, 8), :] = jnp.where(me == 0, 0.0, edge[8:, :])

    def feat_block(b, _):
        L = lanes(b)
        f = []
        for i in range(3):
            acc = pc[i, pl.ds(0, 1), L] * ext[i, pl.ds(8, NT), L]
            for j in range(1, KS):
                acc = acc + pc[i, pl.ds(j, 1), L] * ext[i, pl.ds(8 - j, NT), L]
            f.append(acc.astype(BF16).astype(F32))
        R = pl.ds(pl.multiple_of(b * 128, 128), 128)
        sb[X_U, R, :] = (f[1] * f[2]).T.astype(BF16)
        kf[:, L] = f[1]
        vf[:, L] = f[2]
        qT[R, :] = f[0].T
        return _

    lax.fori_loop(0, NB, feat_block, 0)
    exchange(X_U)

    def sc_block(b, _):
        L = lanes(b)
        R = pl.ds(pl.multiple_of(b * 128, 128), 128)
        scT[R, :] = (ogv[:, L].astype(F32) * gain[pl.ds(b, 1), :]).T
        return _

    lax.fori_loop(0, NB, sc_block, 0)
    for c in loads[3:]:
        c.wait()

    def forward(k, S):
        F[...] = rb[k].astype(F32)

        def pair(g, _):
            x = jnp.concatenate(
                [F[pl.ds(2 * g + e, NP, stride=CH), :] for e in range(2)], axis=1).astype(BF16)
            a = dot(wa[...], jnp.concatenate([x, x], axis=0))
            for e in range(2):
                ar = a[:NP, e * NT:(e + 1) * NT]
                ai = a[NP:, e * NT:(e + 1) * NT]
                br = ar * tr[...] - ai * ti[...]
                bi = ar * ti[...] + ai * tr[...]
                hi, lo = split(jnp.concatenate([br, bi], axis=1))
                R = pl.ds(pl.multiple_of((2 * g + e) * NP, NP), NP)
                bh[R, :] = hi
                bl[R, :] = lo
            return _

        lax.fori_loop(0, CH // 2, pair, 0)

        def block(r, _):
            R = pl.ds(pl.multiple_of(r * 256, 256), 256)
            S[R, :] = (
                dot(bh[R, :], mbh[...]) + dot(bh[R, :], mbl[...]) + dot(bl[R, :], mbh[...]))
            return _

        lax.fori_loop(0, NC // 256, block, 0)

    def inverse(k, A, B, conj):
        def block(r, _):
            R = pl.ds(pl.multiple_of(r * 256, 256), 256)
            a_r, a_i = A[R, pl.ds(0, NT)], A[R, pl.ds(NT, NT)]
            b_r, b_i = B[R, pl.ds(0, NT)], B[R, pl.ds(NT, NT)]
            if conj:
                p_r = a_r * b_r + a_i * b_i
                p_i = a_r * b_i - a_i * b_r
            else:
                p_r = a_r * b_r - a_i * b_i
                p_i = a_r * b_i + a_i * b_r
            hi, lo = split(jnp.concatenate([p_r, p_i], axis=1))
            SP[R, :] = dot(hi, ibh[...]) + dot(hi, ibl[...]) + dot(lo, ibh[...])
            return _

        lax.fori_loop(0, NC // 256, block, 0)

        def pair(g, _):
            cols = []
            for e in range(2):
                R = pl.ds(pl.multiple_of((2 * g + e) * NP, NP), NP)
                cr, ci = SP[R, pl.ds(0, NT)], SP[R, pl.ds(NT, NT)]
                dr = cr * tr[...] + ci * ti[...]
                di = ci * tr[...] - cr * ti[...]
                cols.append(jnp.concatenate([dr, di], axis=0))
            hi, lo = split(jnp.concatenate(cols, axis=1))
            z = dot(ia[...], jnp.concatenate([hi, lo, hi], axis=0))
            for e in range(2):
                F[pl.ds(2 * g + e, NP, stride=CH), :] = z[:, e * NT:(e + 1) * NT]
            return _

        lax.fori_loop(0, CH // 2, pair, 0)
        sb[k] = F[...].astype(BF16)

    arrived(X_H)
    forward(X_H, SH)
    arrived(X_U)
    forward(X_U, SU)
    inverse(X_Z, SU, SH, False)
    exchange(X_Z)
    arrived(X_Z)

    def gate_block(b, carry):
        s1, s2 = carry
        R = pl.ds(pl.multiple_of(b * 128, 128), 128)
        g = qT[R, :] * rb[X_Z, R, :].astype(F32)
        G[R, :] = g
        return s1 + jnp.sum(g * g, axis=0, keepdims=True), s2 + jnp.sum(
            g * scT[R, :], axis=0, keepdims=True)

    zero = jnp.zeros((1, NT), F32)
    s1, s2 = lax.fori_loop(0, NB, gate_block, (zero, zero))
    row = lax.broadcasted_iota(jnp.int32, (8, NT), 0)
    nsb[...] = jnp.where(row == 0, s1, jnp.where(row == 1, s2, 0.0))

    def group_sum(src, dst, ssem, rsem, mine, size, target):
        def one(i, _):
            j = lax.rem(mine + i, size)
            pltpu.make_async_remote_copy(
                src_ref=src, dst_ref=dst.at[mine], send_sem=ssem, recv_sem=rsem,
                device_id=target(j), device_id_type=MESH).start()
            return _

        lax.fori_loop(1, size, one, 0)
        pltpu.make_async_copy(src, dst.at[mine], rsem).start()

    def group_wait(dst, rsem):
        pltpu.make_async_copy(dst, dst, rsem).wait()
        total = dst[0]
        for i in range(1, dst.shape[0]):
            total = total + dst[i]
        return total

    def group_sent(dst, ssem, size):
        part = dst.at[pl.ds(0, size - 1)]
        pltpu.make_async_copy(part, part, ssem).wait()

    group_sum(nsb, nrb, ns, nr, mc, NH, lambda j: {"ch": j})
    tot = group_wait(nrb, nr)
    rs = lax.rsqrt(tot[0:1] / D + EPS)
    inner = rs * tot[1:2] / D
    coef = rs * rs * inner

    def d_block(b, _):
        R = pl.ds(pl.multiple_of(b * 128, 128), 128)
        q = qT[R, :]
        g = G[R, :]
        grad = rs * scT[R, :] - coef * g
        sb[X_D, R, :] = (grad * q).astype(BF16)
        return _

    lax.fori_loop(0, NB, d_block, 0)
    exchange(X_D)

    def out_block(b, _):
        L = lanes(b)
        R = pl.ds(pl.multiple_of(b * 128, 128), 128)
        g = G[R, :]
        normed = (g * rs).T
        out[:, L] = (normed * gain[pl.ds(b, 1), :]).astype(BF16)
        ar1[pl.ds(b, 1), :] = jnp.sum(ogv[:, L].astype(F32) * normed, axis=0, keepdims=True)
        grad = rs * scT[R, :] - coef * g
        gext[0, pl.ds(0, NT), L] = (grad * rb[X_Z, R, :].astype(F32)).T
        return _

    lax.fori_loop(0, NB, out_block, 0)

    def edge_copy(lo, n, s):
        return pltpu.make_async_remote_copy(
            src_ref=gext.at[pl.ds(lo, n), pl.ds(0, 8), :],
            dst_ref=gext.at[pl.ds(lo, n), pl.ds(NT, 8), :],
            send_sem=hs.at[s], recv_sem=hr.at[s], device_id={"ctx": prv}, device_id_type=MESH)

    edge0 = edge_copy(0, 1, 1)
    edge0.start()

    def taps_of(i):
        def block(b, _):
            L = lanes(b)
            g = gext[i, pl.ds(0, NT), L]
            for j in range(KS):
                taps[i, pl.ds(j, 1), L] = jnp.sum(
                    g * ext[i, pl.ds(8 - j, NT), L], axis=0, keepdims=True)
            taps[i, pl.ds(KS, 1), L] = jnp.zeros((1, 128), F32)
            return _

        lax.fori_loop(0, NB, block, 0)
        return lax.dot_general(
            taps[i], member, (((1,), (1,)), ((), ())), preferred_element_type=F32,
            precision=lax.Precision.HIGHEST)

    def short_back(i):
        gext[i, pl.ds(NT, 8), :] = jnp.where(me == NP - 1, 0.0, gext[i, pl.ds(NT, 8), :])

        def block(b, _):
            L = lanes(b)
            acc = pc[i, pl.ds(0, 1), L] * gext[i, pl.ds(0, NT), L]
            for j in range(1, KS):
                acc = acc + pc[i, pl.ds(j, 1), L] * gext[i, pl.ds(j, NT), L]
            pg[i, :, L] = acc.astype(BF16)
            return _

        lax.fori_loop(0, NB, block, 0)

    my_y = lax.rem(me // 2, 8)
    my_zc = (me // 16) * 2 + lax.rem(me, 2)

    def y_peer(j):
        return {"ctx": (me // 16) * 16 + j * 2 + lax.rem(me, 2)}

    def zc_peer(j):
        return {"ctx": (j // 2) * 16 + my_y * 2 + lax.rem(j, 2)}

    t0 = taps_of(0)
    ar1[pl.ds(8, 8), :] = jnp.concatenate([t0, jnp.zeros((8, 128 - NG), F32)], axis=1)
    group_sum(ar1, ar1r, as_.at[0], ar_.at[0], my_y, 8, y_peer)

    arrived(X_D)
    forward(X_D, SD)
    inverse(X_DU, SH, SD, True)
    exchange(X_DU)
    inverse(X_DH, SU, SD, True)
    exchange(X_DH)

    ar1s[...] = group_wait(ar1r, ar_.at[0])
    group_sum(ar1s, ar1q, as_.at[1], ar_.at[1], my_zc, 8, zc_peer)
    edge0.wait()
    short_back(0)

    arrived(X_DU)

    def mix_block(b, _):
        L = lanes(b)
        R = pl.ds(pl.multiple_of(b * 128, 128), 128)
        m = rb[X_DU, R, :].astype(F32).T
        gext[1, pl.ds(0, NT), L] = m * vf[:, L]
        gext[2, pl.ds(0, NT), L] = m * kf[:, L]
        return _

    lax.fori_loop(0, NB, mix_block, 0)
    edge12 = edge_copy(1, 2, 2)
    edge12.start()
    t1 = taps_of(1)
    t2 = taps_of(2)
    ar2[...] = jnp.concatenate([t1, t2], axis=1)
    group_sum(ar2, ar2r, as_.at[2], ar_.at[2], my_y, 8, y_peer)
    edge12.wait()
    short_back(1)
    ar2s[...] = group_wait(ar2r, ar_.at[2])
    group_sum(ar2s, ar2q, as_.at[3], ar_.at[3], my_zc, 8, zc_peer)
    short_back(2)

    arrived(X_DH)

    def filt_block(b, _):
        R = pl.ds(pl.multiple_of(b * 128, 128), 128)
        lg[:, lanes(b)] = rb[X_DH, R, :].astype(F32).T
        return _

    lax.fori_loop(0, NB, filt_block, 0)

    a1 = group_wait(ar1q, ar_.at[1])
    gg[...] = a1[0:8]
    sg[0] = a1[8:8 + KS, 0:NG]
    a2 = group_wait(ar2q, ar_.at[3])
    sg[1] = a2[0:KS, 0:NG]
    sg[2] = a2[0:KS, NG:]

    for k in range(6):
        sent(k)
    group_sent(nrb, ns, NH)
    group_sent(ar1r, as_.at[0], 8)
    group_sent(ar1q, as_.at[1], 8)
    group_sent(ar2r, as_.at[2], 8)
    group_sent(ar2q, as_.at[3], 8)


def on_device(projections, grouped_short_filters, long_filter, norm_gain, out_grad):
    anywhere = pl.BlockSpec(memory_space=pl.ANY)
    vmem = pl.BlockSpec(memory_space=pltpu.VMEM)
    tabs = tables()
    dma = pltpu.SemaphoreType.DMA
    res = pl.pallas_call(
        kernel,
        out_shape=[
            jax.ShapeDtypeStruct((NT, NC), BF16),
            jax.ShapeDtypeStruct((3, NT, NC), BF16),
            jax.ShapeDtypeStruct((3, KS, NG), F32),
            jax.ShapeDtypeStruct((NT, NC), F32),
            jax.ShapeDtypeStruct((8, 128), F32),
        ],
        in_specs=[anywhere, vmem, anywhere, vmem, anywhere] + [anywhere] * 8,
        out_specs=[vmem] * 5,
        scratch_shapes=[
            pltpu.VMEM((3, NT, NC), BF16),
            pltpu.VMEM((NT, NC), F32),
            pltpu.VMEM((NT, NC), BF16),
            *[pltpu.VMEM(t.shape, t.dtype) for t in tabs],
            pltpu.VMEM((3, 16, NC), BF16),
            pltpu.VMEM((3, NT + 8, NC), F32),
            pltpu.VMEM((3, NT + 8, NC), F32),
            pltpu.VMEM((NT, NC), F32),
            pltpu.VMEM((NT, NC), F32),
            pltpu.VMEM((NC, NT), F32),
            pltpu.VMEM((NC, NT), F32),
            pltpu.VMEM((NC, NT), F32),
            pltpu.VMEM((3, 8, NC), F32),
            pltpu.VMEM((3, 8, NC), F32),
            pltpu.VMEM((6, NC, NT), BF16),
            pltpu.VMEM((6, NC, NT), BF16),
            pltpu.VMEM((NC, NT), F32),
            pltpu.VMEM((NC, 2 * NT), BF16),
            pltpu.VMEM((NC, 2 * NT), BF16),
            *[pltpu.VMEM((NC, 2 * NT), F32)] * 4,
            pltpu.VMEM((8, 128), F32),
            pltpu.VMEM((NH, 8, 128), F32),
            pltpu.VMEM((16, 128), F32),
            pltpu.VMEM((8, 16, 128), F32),
            pltpu.VMEM((16, 128), F32),
            pltpu.VMEM((8, 16, 128), F32),
            pltpu.VMEM((8, 128), F32),
            pltpu.VMEM((8, 8, 128), F32),
            pltpu.VMEM((8, 128), F32),
            pltpu.VMEM((8, 8, 128), F32),
            dma((11,)), dma((6,)), dma((6,)), dma((3,)), dma((3,)), dma, dma, dma((4,)), dma((4,)),
        ],
        compiler_params=pltpu.CompilerParams(
            collective_id=0, has_side_effects=True, vmem_limit_bytes=56 * 2**20),
    )(projections, grouped_short_filters, long_filter, norm_gain.reshape(8, 128), out_grad,
      *[jnp.asarray(t) for t in tabs])
    out, pg, sg, lg, gg = res
    return out, pg, sg, lg, gg.reshape(NC)


def solution(mesh):
    in_specs = (P(None, "ctx", "ch"), P(None, None, "ch"), P("ctx", "ch"), P("ch"), P("ctx", "ch"))
    out_specs = (P("ctx", "ch"), P(None, "ctx", "ch"), P(None, None, "ch"), P("ctx", "ch"), P("ch"))
    return jax.shard_map(
        on_device, mesh=mesh, in_specs=in_specs, out_specs=out_specs, check_vma=False
    )
```

```python
import functools
import math

import jax
import jax.numpy as jnp
import numpy as np
from jax import lax
from jax.experimental import pallas as pl
from jax.experimental.pallas import tpu as pltpu
from jax.sharding import PartitionSpec as P

D = 8192
GROUP = 16
KS = 7
EPS = 1e-05
MESH = pl.DeviceIdType.MESH
F32 = jnp.float32
BF16 = jnp.bfloat16

NT = 128
NC = 1024
NP = 64
NH = 8
CH = NC // NP
NB = NC // 128
NG = NC // GROUP
UNP = 4
UNB = 4

X_H, X_U, X_Z, X_D, X_DU, X_DH = range(6)


def split_np(a):
    hi = a.astype(jnp.bfloat16)
    lo = (a - hi.astype(np.float64)).astype(jnp.bfloat16)
    return hi, lo


@functools.lru_cache(maxsize=None)
def tables():
    n1 = np.arange(NP)[None, :]
    k1 = np.arange(NP)[:, None]
    ang = 2 * math.pi * ((n1 * (4 * k1 + 1)) % (4 * NP)) / (4 * NP)
    wa = np.concatenate([np.cos(ang), -np.sin(ang)], axis=0)
    wah, wal = split_np(wa)
    iah, ial = split_np(wa.T / (NP * NT))
    n2 = np.arange(NT)[None, :]
    tw = 2 * math.pi * (n2 * (4 * k1 + 1)) / (4 * NP * NT)
    tr = np.cos(tw).astype(np.float32)
    ti = (-np.sin(tw)).astype(np.float32)
    m = np.arange(NT)
    angb = 2 * math.pi * ((m[:, None] * m[None, :]) % NT) / NT
    c, s = np.cos(angb), np.sin(angb)
    mb = np.block([[c, -s], [s, c]])
    mbh, mbl = split_np(mb)
    ibh, ibl = split_np(mb.T)
    return (
        np.concatenate([wah, wal], axis=1),
        np.concatenate([iah, iah, ial], axis=1),
        mbh, mbl, ibh, ibl, tr, ti,
    )


def split(x):
    hi = x.astype(BF16)
    return hi, (x - hi.astype(F32)).astype(BF16)


def dot(a, b):
    return jnp.dot(a, b, preferred_element_type=F32)


def lanes(b):
    return pl.ds(pl.multiple_of(b * 128, 128), 128)


def kernel(
    proj_hbm, gsf, h_hbm, gain, og_hbm, wa_in, ia_in, mbh_in, mbl_in, ibh_in, ibl_in, tr_in, ti_in,
    out_hbm, pg_hbm, sg, lg_hbm, gg,
    out, pg, lg, out_sem, pv, hv, ogv, wa, ia, mbh, mbl, ibh, ibl, tr, ti,
    halo, ext, gext, kf, vf, qT, scT, G, pc, taps, sb, rb, F, bh, bl, SH, SU, SD, SP,
    nsb, nrb, ar1, ar1r, ar1s, ar1q, ar2, ar2r, ar2s, ar2q,
    in_sem, xs, xr, hs, hr, ns, nr, as_, ar_,
):
    me = lax.axis_index("ctx")
    mc = lax.axis_index("ch")
    bar = pltpu.get_barrier_semaphore()

    loads = [
        pltpu.make_async_copy(a, b, in_sem.at[k])
        for k, (a, b) in enumerate([
            (h_hbm, hv), (proj_hbm, pv), (og_hbm, ogv), (wa_in, wa), (ia_in, ia), (mbh_in, mbh),
            (mbl_in, mbl), (ibh_in, ibh), (ibl_in, ibl), (tr_in, tr), (ti_in, ti)])
    ]
    for c in loads:
        c.start()

    def greet(i, _):
        pl.semaphore_signal(bar, inc=1, device_id={"ctx": lax.rem(me + i, NP)}, device_id_type=MESH)
        return _

    lax.fori_loop(1, NP, greet, 0)

    def greet_ch(i, _):
        pl.semaphore_signal(bar, inc=1, device_id={"ch": lax.rem(mc + i, NH)}, device_id_type=MESH)
        return _

    lax.fori_loop(1, NH, greet_ch, 0)

    def rows16(i):
        return pl.ds(pl.multiple_of(i * CH, CH), CH)

    def send_to(k, t):
        return pltpu.make_async_remote_copy(
            src_ref=sb.at[k, rows16(t)], dst_ref=rb.at[k, rows16(me)],
            send_sem=xs.at[k], recv_sem=xr.at[k], device_id={"ctx": t}, device_id_type=MESH)

    my_z = me // 16
    my_half = lax.rem(me // 8, 2)

    def exchange(k, fill):
        def block(i, _):
            z = jnp.bitwise_xor(my_z, 3 - i // 2)
            half = jnp.where(lax.rem(i, 2) == 0, 1 - my_half, my_half)
            b = 2 * z + half
            fill(b, pl.ds(pl.multiple_of(b * 128, 128), 128))

            def one(j, _):
                send_to(k, b * 8 + lax.rem(me + j, 8)).start()
                return _

            lax.fori_loop(jnp.where(i == NB - 1, 1, 0), 8, one, 0)
            return _

        lax.fori_loop(0, NB, block, 0)
        pltpu.make_async_copy(sb.at[k, rows16(me)], rb.at[k, rows16(me)], xr.at[k]).start()

    def arrived(k):
        pltpu.make_async_copy(rb.at[k], rb.at[k], xr.at[k]).wait()

    def sent(k):
        part = sb.at[k, pl.ds(0, NC - CH)]
        pltpu.make_async_copy(part, part, xs.at[k]).wait()

    loads[0].wait()

    def h_block(b, R):
        sb[X_H, R, :] = hv[:, lanes(b)].T.astype(BF16)

    loads[1].wait()

    pl.semaphore_wait(bar, NP - 1 + NH - 1)

    nxt = lax.rem(me + 1, NP)
    prv = lax.rem(me + NP - 1, NP)
    halo_copy = pltpu.make_async_remote_copy(
        src_ref=pv.at[:, pl.ds(NT - 16, 16), :], dst_ref=halo, send_sem=hs.at[0], recv_sem=hr.at[0],
        device_id={"ctx": nxt}, device_id_type=MESH)
    halo_copy.start()
    exchange(X_H, h_block)

    member = (
        lax.broadcasted_iota(jnp.int32, (NG, NC), 1) // GROUP
        == lax.broadcasted_iota(jnp.int32, (NG, NC), 0)
    ).astype(F32)
    for i in range(3):
        pc[i, pl.ds(0, KS), :] = jnp.dot(
            gsf[i], member, preferred_element_type=F32, precision=lax.Precision.HIGHEST)
        ext[i, pl.ds(8, NT), :] = pv[i].astype(F32)
    loads[2].wait()

    halo_copy.wait()
    for i in range(3):
        edge = halo[i].astype(F32)
        ext[i, pl.ds(0, 8), :] = jnp.where(me == 0, 0.0, edge[8:, :])

    def feat_block(b, R):
        L = lanes(b)
        f = []
        for i in range(3):
            acc = pc[i, pl.ds(0, 1), L] * ext[i, pl.ds(8, NT), L]
            for j in range(1, KS):
                acc = acc + pc[i, pl.ds(j, 1), L] * ext[i, pl.ds(8 - j, NT), L]
            f.append(acc.astype(BF16).astype(F32))
        sb[X_U, R, :] = (f[1] * f[2]).T.astype(BF16)
        kf[:, L] = f[1]
        vf[:, L] = f[2]
        qT[R, :] = f[0].T

    exchange(X_U, feat_block)

    def sc_block(b, _):
        L = lanes(b)
        R = pl.ds(pl.multiple_of(b * 128, 128), 128)
        scT[R, :] = (ogv[:, L].astype(F32) * gain[pl.ds(b, 1), :]).T
        return _

    lax.fori_loop(0, NB, sc_block, 0)
    for c in loads[3:]:
        c.wait()

    def forward(k, S):
        F[...] = rb[k].astype(F32)

        def pair(g, _):
            x = jnp.concatenate(
                [F[pl.ds(2 * g + e, NP, stride=CH), :] for e in range(2)], axis=1).astype(BF16)
            a = dot(wa[...], jnp.concatenate([x, x], axis=0))
            for e in range(2):
                ar = a[:NP, e * NT:(e + 1) * NT]
                ai = a[NP:, e * NT:(e + 1) * NT]
                br = ar * tr[...] - ai * ti[...]
                bi = ar * ti[...] + ai * tr[...]
                hi, lo = split(jnp.concatenate([br, bi], axis=1))
                R = pl.ds(pl.multiple_of((2 * g + e) * NP, NP), NP)
                bh[R, :] = hi
                bl[R, :] = lo
            return _

        lax.fori_loop(0, CH // 2, pair, 0, unroll=UNP)

        def block(r, _):
            R = pl.ds(pl.multiple_of(r * 256, 256), 256)
            S[R, :] = (
                dot(bh[R, :], mbh[...]) + dot(bh[R, :], mbl[...]) + dot(bl[R, :], mbh[...]))
            return _

        lax.fori_loop(0, NC // 256, block, 0, unroll=UNB)

    def inverse(k, A, B, conj):
        def block(r, _):
            R = pl.ds(pl.multiple_of(r * 256, 256), 256)
            a_r, a_i = A[R, pl.ds(0, NT)], A[R, pl.ds(NT, NT)]
            b_r, b_i = B[R, pl.ds(0, NT)], B[R, pl.ds(NT, NT)]
            if conj:
                p_r = a_r * b_r + a_i * b_i
                p_i = a_r * b_i - a_i * b_r
            else:
                p_r = a_r * b_r - a_i * b_i
                p_i = a_r * b_i + a_i * b_r
            hi, lo = split(jnp.concatenate([p_r, p_i], axis=1))
            SP[R, :] = dot(hi, ibh[...]) + dot(hi, ibl[...]) + dot(lo, ibh[...])
            return _

        lax.fori_loop(0, NC // 256, block, 0, unroll=UNB)

        def pair(g, _):
            cols = []
            for e in range(2):
                R = pl.ds(pl.multiple_of((2 * g + e) * NP, NP), NP)
                cr, ci = SP[R, pl.ds(0, NT)], SP[R, pl.ds(NT, NT)]
                dr = cr * tr[...] + ci * ti[...]
                di = ci * tr[...] - cr * ti[...]
                cols.append(jnp.concatenate([dr, di], axis=0))
            hi, lo = split(jnp.concatenate(cols, axis=1))
            z = dot(ia[...], jnp.concatenate([hi, lo, hi], axis=0))
            for e in range(2):
                F[pl.ds(2 * g + e, NP, stride=CH), :] = z[:, e * NT:(e + 1) * NT]
            return _

        lax.fori_loop(0, CH // 2, pair, 0, unroll=UNP)

        def fill(b, R):
            sb[k, R, :] = F[R, :].astype(BF16)

        exchange(k, fill)

    arrived(X_H)
    forward(X_H, SH)
    arrived(X_U)
    forward(X_U, SU)
    inverse(X_Z, SU, SH, False)
    arrived(X_Z)

    def gate_block(b, carry):
        s1, s2 = carry
        R = pl.ds(pl.multiple_of(b * 128, 128), 128)
        g = qT[R, :] * rb[X_Z, R, :].astype(F32)
        G[R, :] = g
        return s1 + jnp.sum(g * g, axis=0, keepdims=True), s2 + jnp.sum(
            g * scT[R, :], axis=0, keepdims=True)

    zero = jnp.zeros((1, NT), F32)
    s1, s2 = lax.fori_loop(0, NB, gate_block, (zero, zero))
    row = lax.broadcasted_iota(jnp.int32, (8, NT), 0)
    nsb[...] = jnp.where(row == 0, s1, jnp.where(row == 1, s2, 0.0))

    def group_sum(src, dst, ssem, rsem, mine, size, target):
        def one(i, _):
            j = lax.rem(mine + i, size)
            pltpu.make_async_remote_copy(
                src_ref=src, dst_ref=dst.at[mine], send_sem=ssem, recv_sem=rsem,
                device_id=target(j), device_id_type=MESH).start()
            return _

        lax.fori_loop(1, size, one, 0)
        pltpu.make_async_copy(src, dst.at[mine], rsem).start()

    def group_wait(dst, rsem):
        pltpu.make_async_copy(dst, dst, rsem).wait()
        total = dst[0]
        for i in range(1, dst.shape[0]):
            total = total + dst[i]
        return total

    def group_sent(dst, ssem, size):
        part = dst.at[pl.ds(0, size - 1)]
        pltpu.make_async_copy(part, part, ssem).wait()

    group_sum(nsb, nrb, ns, nr, mc, NH, lambda j: {"ch": j})
    tot = group_wait(nrb, nr)
    rs = lax.rsqrt(tot[0:1] / D + EPS)
    inner = rs * tot[1:2] / D
    coef = rs * rs * inner

    def d_block(b, R):
        q = qT[R, :]
        g = G[R, :]
        grad = rs * scT[R, :] - coef * g
        sb[X_D, R, :] = (grad * q).astype(BF16)

    exchange(X_D, d_block)

    def out_block(b, _):
        L = lanes(b)
        R = pl.ds(pl.multiple_of(b * 128, 128), 128)
        g = G[R, :]
        normed = (g * rs).T
        out[:, L] = (normed * gain[pl.ds(b, 1), :]).astype(BF16)
        ar1[pl.ds(b, 1), :] = jnp.sum(ogv[:, L].astype(F32) * normed, axis=0, keepdims=True)
        grad = rs * scT[R, :] - coef * g
        gext[0, pl.ds(0, NT), L] = (grad * rb[X_Z, R, :].astype(F32)).T
        return _

    lax.fori_loop(0, NB, out_block, 0)

    def edge_copy(lo, n, s):
        return pltpu.make_async_remote_copy(
            src_ref=gext.at[pl.ds(lo, n), pl.ds(0, 8), :],
            dst_ref=gext.at[pl.ds(lo, n), pl.ds(NT, 8), :],
            send_sem=hs.at[s], recv_sem=hr.at[s], device_id={"ctx": prv}, device_id_type=MESH)

    stores = [pltpu.make_async_copy(out, out_hbm, out_sem.at[0])]
    stores += [pltpu.make_async_copy(pg.at[i], pg_hbm.at[i], out_sem.at[1 + i]) for i in range(3)]
    stores[0].start()
    edge0 = edge_copy(0, 1, 1)
    edge0.start()

    def taps_of(i):
        def block(b, _):
            L = lanes(b)
            g = gext[i, pl.ds(0, NT), L]
            for j in range(KS):
                taps[i, pl.ds(j, 1), L] = jnp.sum(
                    g * ext[i, pl.ds(8 - j, NT), L], axis=0, keepdims=True)
            taps[i, pl.ds(KS, 1), L] = jnp.zeros((1, 128), F32)
            return _

        lax.fori_loop(0, NB, block, 0)
        return lax.dot_general(
            taps[i], member, (((1,), (1,)), ((), ())), preferred_element_type=F32,
            precision=lax.Precision.HIGHEST)

    def short_back(i):
        gext[i, pl.ds(NT, 8), :] = jnp.where(me == NP - 1, 0.0, gext[i, pl.ds(NT, 8), :])

        def block(b, _):
            L = lanes(b)
            acc = pc[i, pl.ds(0, 1), L] * gext[i, pl.ds(0, NT), L]
            for j in range(1, KS):
                acc = acc + pc[i, pl.ds(j, 1), L] * gext[i, pl.ds(j, NT), L]
            pg[i, :, L] = acc.astype(BF16)
            return _

        lax.fori_loop(0, NB, block, 0)
        stores[1 + i].start()

    my_y = lax.rem(me // 2, 8)
    my_zc = (me // 16) * 2 + lax.rem(me, 2)

    def y_peer(j):
        return {"ctx": (me // 16) * 16 + j * 2 + lax.rem(me, 2)}

    def zc_peer(j):
        return {"ctx": (j // 2) * 16 + my_y * 2 + lax.rem(j, 2)}

    t0 = taps_of(0)
    ar1[pl.ds(8, 8), :] = jnp.concatenate([t0, jnp.zeros((8, 128 - NG), F32)], axis=1)
    group_sum(ar1, ar1r, as_.at[0], ar_.at[0], my_y, 8, y_peer)

    arrived(X_D)
    forward(X_D, SD)
    inverse(X_DU, SH, SD, True)
    inverse(X_DH, SU, SD, True)

    ar1s[...] = group_wait(ar1r, ar_.at[0])
    group_sum(ar1s, ar1q, as_.at[1], ar_.at[1], my_zc, 8, zc_peer)
    edge0.wait()
    short_back(0)

    arrived(X_DU)

    def mix_block(b, _):
        L = lanes(b)
        R = pl.ds(pl.multiple_of(b * 128, 128), 128)
        m = rb[X_DU, R, :].astype(F32).T
        gext[1, pl.ds(0, NT), L] = m * vf[:, L]
        gext[2, pl.ds(0, NT), L] = m * kf[:, L]
        return _

    lax.fori_loop(0, NB, mix_block, 0)
    edge12 = edge_copy(1, 2, 2)
    edge12.start()
    t1 = taps_of(1)
    t2 = taps_of(2)
    ar2[...] = jnp.concatenate([t1, t2], axis=1)
    group_sum(ar2, ar2r, as_.at[2], ar_.at[2], my_y, 8, y_peer)
    edge12.wait()
    short_back(1)
    ar2s[...] = group_wait(ar2r, ar_.at[2])
    group_sum(ar2s, ar2q, as_.at[3], ar_.at[3], my_zc, 8, zc_peer)
    short_back(2)

    arrived(X_DH)

    def filt_block(b, _):
        R = pl.ds(pl.multiple_of(b * 128, 128), 128)
        lg[:, lanes(b)] = rb[X_DH, R, :].astype(F32).T
        return _

    lax.fori_loop(0, NB, filt_block, 0)
    stores.append(pltpu.make_async_copy(lg, lg_hbm, out_sem.at[4]))
    stores[4].start()

    a1 = group_wait(ar1q, ar_.at[1])
    gg[...] = a1[0:8]
    sg[0] = a1[8:8 + KS, 0:NG]
    a2 = group_wait(ar2q, ar_.at[3])
    sg[1] = a2[0:KS, 0:NG]
    sg[2] = a2[0:KS, NG:]

    for c in stores:
        c.wait()
    for k in range(6):
        sent(k)
    group_sent(nrb, ns, NH)
    group_sent(ar1r, as_.at[0], 8)
    group_sent(ar1q, as_.at[1], 8)
    group_sent(ar2r, as_.at[2], 8)
    group_sent(ar2q, as_.at[3], 8)


def hand_over(*refs):
    ins, outs, bufs, sem = refs[:5], refs[5:10], refs[10:15], refs[15]
    first = [pltpu.make_async_copy(a, b, sem.at[i]) for i, (a, b) in enumerate(zip(ins, bufs))]
    last = [pltpu.make_async_copy(b, c, sem.at[5 + i]) for i, (b, c) in enumerate(zip(bufs, outs))]
    for c in first:
        c.start()
    for a, c in zip(first, last):
        a.wait()
        c.start()
    for c in last:
        c.wait()


def on_device(projections, grouped_short_filters, long_filter, norm_gain, out_grad):
    anywhere = pl.BlockSpec(memory_space=pl.ANY)
    vmem = pl.BlockSpec(memory_space=pltpu.VMEM)
    tabs = tables()
    dma = pltpu.SemaphoreType.DMA
    res = pl.pallas_call(
        kernel,
        out_shape=[
            jax.ShapeDtypeStruct((NT, NC), BF16),
            jax.ShapeDtypeStruct((3, NT, NC), BF16),
            jax.ShapeDtypeStruct((3, KS, NG), F32),
            jax.ShapeDtypeStruct((NT, NC), F32),
            jax.ShapeDtypeStruct((8, 128), F32),
        ],
        in_specs=[anywhere, vmem, anywhere, vmem, anywhere] + [anywhere] * 8,
        out_specs=[anywhere, anywhere, vmem, anywhere, vmem],
        scratch_shapes=[
            pltpu.VMEM((NT, NC), BF16),
            pltpu.VMEM((3, NT, NC), BF16),
            pltpu.VMEM((NT, NC), F32),
            dma((5,)),
            pltpu.VMEM((3, NT, NC), BF16),
            pltpu.VMEM((NT, NC), F32),
            pltpu.VMEM((NT, NC), BF16),
            *[pltpu.VMEM(t.shape, t.dtype) for t in tabs],
            pltpu.VMEM((3, 16, NC), BF16),
            pltpu.VMEM((3, NT + 8, NC), F32),
            pltpu.VMEM((3, NT + 8, NC), F32),
            pltpu.VMEM((NT, NC), F32),
            pltpu.VMEM((NT, NC), F32),
            pltpu.VMEM((NC, NT), F32),
            pltpu.VMEM((NC, NT), F32),
            pltpu.VMEM((NC, NT), F32),
            pltpu.VMEM((3, 8, NC), F32),
            pltpu.VMEM((3, 8, NC), F32),
            pltpu.VMEM((6, NC, NT), BF16),
            pltpu.VMEM((6, NC, NT), BF16),
            pltpu.VMEM((NC, NT), F32),
            pltpu.VMEM((NC, 2 * NT), BF16),
            pltpu.VMEM((NC, 2 * NT), BF16),
            *[pltpu.VMEM((NC, 2 * NT), F32)] * 4,
            pltpu.VMEM((8, 128), F32),
            pltpu.VMEM((NH, 8, 128), F32),
            pltpu.VMEM((16, 128), F32),
            pltpu.VMEM((8, 16, 128), F32),
            pltpu.VMEM((16, 128), F32),
            pltpu.VMEM((8, 16, 128), F32),
            pltpu.VMEM((8, 128), F32),
            pltpu.VMEM((8, 8, 128), F32),
            pltpu.VMEM((8, 128), F32),
            pltpu.VMEM((8, 8, 128), F32),
            dma((11,)), dma((6,)), dma((6,)), dma((3,)), dma((3,)), dma, dma, dma((4,)), dma((4,)),
        ],
        compiler_params=pltpu.CompilerParams(
            collective_id=0, has_side_effects=True, vmem_limit_bytes=56 * 2**20),
    )(projections, grouped_short_filters, long_filter, norm_gain.reshape(8, 128), out_grad,
      *[jnp.asarray(t) for t in tabs])
    out, pg, sg, lg, gg = pl.pallas_call(
        hand_over,
        out_shape=[jax.ShapeDtypeStruct(r.shape, r.dtype) for r in res],
        in_specs=[anywhere] * 5,
        out_specs=[anywhere] * 5,
        scratch_shapes=[*[pltpu.VMEM(r.shape, r.dtype) for r in res], dma((10,))],
    )(*res)
    return out, pg, sg, lg, gg.reshape(NC)


def solution(mesh):
    in_specs = (P(None, "ctx", "ch"), P(None, None, "ch"), P("ctx", "ch"), P("ch"), P("ctx", "ch"))
    out_specs = (P("ctx", "ch"), P(None, "ctx", "ch"), P(None, None, "ch"), P("ctx", "ch"), P("ch"))
    return jax.shard_map(
        on_device, mesh=mesh, in_specs=in_specs, out_specs=out_specs, check_vma=False
    )
```

```python
import functools
import math

import jax
import jax.numpy as jnp
import numpy as np
from jax import lax
from jax.experimental import pallas as pl
from jax.experimental.pallas import tpu as pltpu
from jax.sharding import PartitionSpec as P

D = 8192
GROUP = 16
KS = 7
EPS = 1e-05
MESH = pl.DeviceIdType.MESH
F32 = jnp.float32
BF16 = jnp.bfloat16

NT = 128
NC = 1024
NP = 64
NH = 8
CH = NC // NP
NB = NC // 128
NG = NC // GROUP
UNP = 8
UNB = 4

X_H, X_U, X_Z, X_D, X_DU, X_DH = range(6)


def split_np(a):
    hi = a.astype(jnp.bfloat16)
    lo = (a - hi.astype(np.float64)).astype(jnp.bfloat16)
    return hi, lo


@functools.lru_cache(maxsize=None)
def tables():
    n1 = np.arange(NP)[None, :]
    k1 = np.arange(NP)[:, None]
    ang = 2 * math.pi * ((n1 * (4 * k1 + 1)) % (4 * NP)) / (4 * NP)
    wa = np.concatenate([np.cos(ang), -np.sin(ang)], axis=0)
    wah, wal = split_np(wa)
    iah, ial = split_np(wa.T / (NP * NT))
    n2 = np.arange(NT)[None, :]
    tw = 2 * math.pi * (n2 * (4 * k1 + 1)) / (4 * NP * NT)
    tr = np.cos(tw).astype(np.float32)
    ti = (-np.sin(tw)).astype(np.float32)
    m = np.arange(NT)
    angb = 2 * math.pi * ((m[:, None] * m[None, :]) % NT) / NT
    c, s = np.cos(angb), np.sin(angb)
    mb = np.block([[c, -s], [s, c]])
    mbh, mbl = split_np(mb)
    ibh, ibl = split_np(mb.T)
    return (
        np.concatenate([wah, wal], axis=1),
        np.concatenate([iah, iah, ial], axis=1),
        mbh, mbl, ibh, ibl, tr, ti,
    )


def split(x):
    hi = x.astype(BF16)
    return hi, (x - hi.astype(F32)).astype(BF16)


def dot(a, b):
    return jnp.dot(a, b, preferred_element_type=F32)


def lanes(b):
    return pl.ds(pl.multiple_of(b * 128, 128), 128)


def kernel(
    proj_hbm, gsf, h_hbm, gain, og_hbm, wa_in, ia_in, mbh_in, mbl_in, ibh_in, ibl_in, tr_in, ti_in,
    out_hbm, pg_hbm, sg, lg_hbm, gg,
    out, pg, lg, out_sem, pv, hv, ogv, wa, ia, mbh, mbl, ibh, ibl, tr, ti,
    halo, ext, gext, kf, vf, qT, scT, G, pc, taps, sb, rb, F, bh, bl, SH, SU, SD, SP,
    nsb, nrb, ar1, ar1r, ar1s, ar1q, ar2, ar2r, ar2s, ar2q,
    in_sem, xs, xr, hs, hr, ns, nr, as_, ar_,
):
    me = lax.axis_index("ctx")
    mc = lax.axis_index("ch")
    bar = pltpu.get_barrier_semaphore()

    loads = [
        pltpu.make_async_copy(a, b, in_sem.at[k])
        for k, (a, b) in enumerate([
            (h_hbm, hv), (proj_hbm, pv), (og_hbm, ogv), (wa_in, wa), (ia_in, ia), (mbh_in, mbh),
            (mbl_in, mbl), (ibh_in, ibh), (ibl_in, ibl), (tr_in, tr), (ti_in, ti)])
    ]
    for c in loads:
        c.start()

    def greet(i, _):
        pl.semaphore_signal(bar, inc=1, device_id={"ctx": lax.rem(me + i, NP)}, device_id_type=MESH)
        return _

    lax.fori_loop(1, NP, greet, 0)

    def greet_ch(i, _):
        pl.semaphore_signal(bar, inc=1, device_id={"ch": lax.rem(mc + i, NH)}, device_id_type=MESH)
        return _

    lax.fori_loop(1, NH, greet_ch, 0)

    def rows16(i):
        return pl.ds(pl.multiple_of(i * CH, CH), CH)

    def send_to(k, t):
        return pltpu.make_async_remote_copy(
            src_ref=sb.at[k, rows16(t)], dst_ref=rb.at[k, rows16(me)],
            send_sem=xs.at[k], recv_sem=xr.at[k], device_id={"ctx": t}, device_id_type=MESH)

    my_z = me // 16
    my_half = lax.rem(me // 8, 2)

    def exchange(k, fill):
        def block(i, _):
            z = jnp.bitwise_xor(my_z, 3 - i // 2)
            half = jnp.where(lax.rem(i, 2) == 0, 1 - my_half, my_half)
            b = 2 * z + half
            fill(b, pl.ds(pl.multiple_of(b * 128, 128), 128))

            def one(j, _):
                send_to(k, b * 8 + lax.rem(me + j, 8)).start()
                return _

            lax.fori_loop(jnp.where(i == NB - 1, 1, 0), 8, one, 0)
            return _

        lax.fori_loop(0, NB, block, 0)
        pltpu.make_async_copy(sb.at[k, rows16(me)], rb.at[k, rows16(me)], xr.at[k]).start()

    def arrived(k):
        pltpu.make_async_copy(rb.at[k], rb.at[k], xr.at[k]).wait()

    def sent(k):
        part = sb.at[k, pl.ds(0, NC - CH)]
        pltpu.make_async_copy(part, part, xs.at[k]).wait()

    member = (
        lax.broadcasted_iota(jnp.int32, (NG, NC), 1) // GROUP
        == lax.broadcasted_iota(jnp.int32, (NG, NC), 0)
    ).astype(F32)
    loads[1].wait()
    for i in range(3):
        pc[i, pl.ds(0, KS), :] = jnp.dot(
            gsf[i], member, preferred_element_type=F32, precision=lax.Precision.HIGHEST)
        ext[i, pl.ds(8, NT), :] = pv[i].astype(F32)

    loads[0].wait()
    for b in range(NB):
        sb[X_H, pl.ds(b * 128, 128), :] = hv[:, pl.ds(b * 128, 128)].T.astype(BF16)

    pl.semaphore_wait(bar, NP - 1 + NH - 1)

    nxt = lax.rem(me + 1, NP)
    prv = lax.rem(me + NP - 1, NP)
    halo_copy = pltpu.make_async_remote_copy(
        src_ref=pv.at[:, pl.ds(NT - 16, 16), :], dst_ref=halo, send_sem=hs.at[0], recv_sem=hr.at[0],
        device_id={"ctx": nxt}, device_id_type=MESH)
    halo_copy.start()
    exchange(X_H, lambda b, R: None)

    halo_copy.wait()
    for i in range(3):
        edge = halo[i].astype(F32)
        ext[i, pl.ds(0, 8), :] = jnp.where(me == 0, 0.0, edge[8:, :])

    def feat_block(b, R):
        L = lanes(b)
        f = []
        for i in range(3):
            acc = pc[i, pl.ds(0, 1), L] * ext[i, pl.ds(8, NT), L]
            for j in range(1, KS):
                acc = acc + pc[i, pl.ds(j, 1), L] * ext[i, pl.ds(8 - j, NT), L]
            f.append(acc.astype(BF16).astype(F32))
        sb[X_U, R, :] = (f[1] * f[2]).T.astype(BF16)
        kf[:, L] = f[1]
        vf[:, L] = f[2]
        qT[R, :] = f[0].T

    exchange(X_U, feat_block)

    loads[2].wait()

    def sc_block(b, _):
        L = lanes(b)
        R = pl.ds(pl.multiple_of(b * 128, 128), 128)
        scT[R, :] = (ogv[:, L].astype(F32) * gain[pl.ds(b, 1), :]).T
        return _

    lax.fori_loop(0, NB, sc_block, 0)
    for c in loads[3:]:
        c.wait()

    def forward(k, S):
        F[...] = rb[k].astype(F32)

        def pair(g, _):
            x = jnp.concatenate(
                [F[pl.ds(2 * g + e, NP, stride=CH), :] for e in range(2)], axis=1).astype(BF16)
            a = dot(wa[...], jnp.concatenate([x, x], axis=0))
            for e in range(2):
                ar = a[:NP, e * NT:(e + 1) * NT]
                ai = a[NP:, e * NT:(e + 1) * NT]
                br = ar * tr[...] - ai * ti[...]
                bi = ar * ti[...] + ai * tr[...]
                hi, lo = split(jnp.concatenate([br, bi], axis=1))
                R = pl.ds(pl.multiple_of((2 * g + e) * NP, NP), NP)
                bh[R, :] = hi
                bl[R, :] = lo
            return _

        lax.fori_loop(0, CH // 2, pair, 0, unroll=UNP)

        def block(r, _):
            R = pl.ds(pl.multiple_of(r * 256, 256), 256)
            S[R, :] = (
                dot(bh[R, :], mbh[...]) + dot(bh[R, :], mbl[...]) + dot(bl[R, :], mbh[...]))
            return _

        lax.fori_loop(0, NC // 256, block, 0, unroll=UNB)

    def inverse(k, A, B, conj):
        def block(r, _):
            R = pl.ds(pl.multiple_of(r * 256, 256), 256)
            a_r, a_i = A[R, pl.ds(0, NT)], A[R, pl.ds(NT, NT)]
            b_r, b_i = B[R, pl.ds(0, NT)], B[R, pl.ds(NT, NT)]
            if conj:
                p_r = a_r * b_r + a_i * b_i
                p_i = a_r * b_i - a_i * b_r
            else:
                p_r = a_r * b_r - a_i * b_i
                p_i = a_r * b_i + a_i * b_r
            hi, lo = split(jnp.concatenate([p_r, p_i], axis=1))
            SP[R, :] = dot(hi, ibh[...]) + dot(hi, ibl[...]) + dot(lo, ibh[...])
            return _

        lax.fori_loop(0, NC // 256, block, 0, unroll=UNB)

        def pair(g, _):
            cols = []
            for e in range(2):
                R = pl.ds(pl.multiple_of((2 * g + e) * NP, NP), NP)
                cr, ci = SP[R, pl.ds(0, NT)], SP[R, pl.ds(NT, NT)]
                dr = cr * tr[...] + ci * ti[...]
                di = ci * tr[...] - cr * ti[...]
                cols.append(jnp.concatenate([dr, di], axis=0))
            hi, lo = split(jnp.concatenate(cols, axis=1))
            z = dot(ia[...], jnp.concatenate([hi, lo, hi], axis=0))
            for e in range(2):
                F[pl.ds(2 * g + e, NP, stride=CH), :] = z[:, e * NT:(e + 1) * NT]
            return _

        lax.fori_loop(0, CH // 2, pair, 0, unroll=UNP)

        def fill(b, R):
            sb[k, R, :] = F[R, :].astype(BF16)

        exchange(k, fill)

    arrived(X_H)
    forward(X_H, SH)
    arrived(X_U)
    forward(X_U, SU)
    inverse(X_Z, SU, SH, False)
    arrived(X_Z)

    def gate_block(b, carry):
        s1, s2 = carry
        R = pl.ds(pl.multiple_of(b * 128, 128), 128)
        g = qT[R, :] * rb[X_Z, R, :].astype(F32)
        G[R, :] = g
        return s1 + jnp.sum(g * g, axis=0, keepdims=True), s2 + jnp.sum(
            g * scT[R, :], axis=0, keepdims=True)

    zero = jnp.zeros((1, NT), F32)
    s1, s2 = lax.fori_loop(0, NB, gate_block, (zero, zero))
    row = lax.broadcasted_iota(jnp.int32, (8, NT), 0)
    nsb[...] = jnp.where(row == 0, s1, jnp.where(row == 1, s2, 0.0))

    def group_sum(src, dst, ssem, rsem, mine, size, target):
        def one(i, _):
            j = lax.rem(mine + i, size)
            pltpu.make_async_remote_copy(
                src_ref=src, dst_ref=dst.at[mine], send_sem=ssem, recv_sem=rsem,
                device_id=target(j), device_id_type=MESH).start()
            return _

        lax.fori_loop(1, size, one, 0)
        pltpu.make_async_copy(src, dst.at[mine], rsem).start()

    def group_wait(dst, rsem):
        pltpu.make_async_copy(dst, dst, rsem).wait()
        total = dst[0]
        for i in range(1, dst.shape[0]):
            total = total + dst[i]
        return total

    def group_sent(dst, ssem, size):
        part = dst.at[pl.ds(0, size - 1)]
        pltpu.make_async_copy(part, part, ssem).wait()

    group_sum(nsb, nrb, ns, nr, mc, NH, lambda j: {"ch": j})
    tot = group_wait(nrb, nr)
    rs = lax.rsqrt(tot[0:1] / D + EPS)
    inner = rs * tot[1:2] / D
    coef = rs * rs * inner

    def d_block(b, R):
        q = qT[R, :]
        g = G[R, :]
        grad = rs * scT[R, :] - coef * g
        sb[X_D, R, :] = (grad * q).astype(BF16)

    exchange(X_D, d_block)

    def out_block(b, _):
        L = lanes(b)
        R = pl.ds(pl.multiple_of(b * 128, 128), 128)
        g = G[R, :]
        normed = (g * rs).T
        out[:, L] = (normed * gain[pl.ds(b, 1), :]).astype(BF16)
        ar1[pl.ds(b, 1), :] = jnp.sum(ogv[:, L].astype(F32) * normed, axis=0, keepdims=True)
        grad = rs * scT[R, :] - coef * g
        gext[0, pl.ds(0, NT), L] = (grad * rb[X_Z, R, :].astype(F32)).T
        return _

    lax.fori_loop(0, NB, out_block, 0)

    def edge_copy(lo, n, s):
        return pltpu.make_async_remote_copy(
            src_ref=gext.at[pl.ds(lo, n), pl.ds(0, 8), :],
            dst_ref=gext.at[pl.ds(lo, n), pl.ds(NT, 8), :],
            send_sem=hs.at[s], recv_sem=hr.at[s], device_id={"ctx": prv}, device_id_type=MESH)

    stores = [pltpu.make_async_copy(out, out_hbm, out_sem.at[0])]
    stores += [pltpu.make_async_copy(pg.at[i], pg_hbm.at[i], out_sem.at[1 + i]) for i in range(3)]
    stores[0].start()
    edge0 = edge_copy(0, 1, 1)
    edge0.start()

    def taps_of(i):
        def block(b, _):
            L = lanes(b)
            g = gext[i, pl.ds(0, NT), L]
            for j in range(KS):
                taps[i, pl.ds(j, 1), L] = jnp.sum(
                    g * ext[i, pl.ds(8 - j, NT), L], axis=0, keepdims=True)
            taps[i, pl.ds(KS, 1), L] = jnp.zeros((1, 128), F32)
            return _

        lax.fori_loop(0, NB, block, 0, unroll=2)
        return lax.dot_general(
            taps[i], member, (((1,), (1,)), ((), ())), preferred_element_type=F32,
            precision=lax.Precision.HIGHEST)

    def short_back(i):
        gext[i, pl.ds(NT, 8), :] = jnp.where(me == NP - 1, 0.0, gext[i, pl.ds(NT, 8), :])

        def block(b, _):
            L = lanes(b)
            acc = pc[i, pl.ds(0, 1), L] * gext[i, pl.ds(0, NT), L]
            for j in range(1, KS):
                acc = acc + pc[i, pl.ds(j, 1), L] * gext[i, pl.ds(j, NT), L]
            pg[i, :, L] = acc.astype(BF16)
            return _

        lax.fori_loop(0, NB, block, 0)
        stores[1 + i].start()

    my_y = lax.rem(me // 2, 8)
    my_zc = (me // 16) * 2 + lax.rem(me, 2)

    def y_peer(j):
        return {"ctx": (me // 16) * 16 + j * 2 + lax.rem(me, 2)}

    def zc_peer(j):
        return {"ctx": (j // 2) * 16 + my_y * 2 + lax.rem(j, 2)}

    t0 = taps_of(0)
    ar1[pl.ds(8, 8), :] = jnp.concatenate([t0, jnp.zeros((8, 128 - NG), F32)], axis=1)
    group_sum(ar1, ar1r, as_.at[0], ar_.at[0], my_y, 8, y_peer)

    arrived(X_D)
    forward(X_D, SD)
    inverse(X_DU, SH, SD, True)
    inverse(X_DH, SU, SD, True)

    ar1s[...] = group_wait(ar1r, ar_.at[0])
    group_sum(ar1s, ar1q, as_.at[1], ar_.at[1], my_zc, 8, zc_peer)
    edge0.wait()
    short_back(0)

    arrived(X_DU)

    def mix_block(b, _):
        L = lanes(b)
        R = pl.ds(pl.multiple_of(b * 128, 128), 128)
        m = rb[X_DU, R, :].astype(F32).T
        gext[1, pl.ds(0, NT), L] = m * vf[:, L]
        gext[2, pl.ds(0, NT), L] = m * kf[:, L]
        return _

    lax.fori_loop(0, NB, mix_block, 0, unroll=4)
    edge12 = edge_copy(1, 2, 2)
    edge12.start()
    t1 = taps_of(1)
    t2 = taps_of(2)
    ar2[...] = jnp.concatenate([t1, t2], axis=1)
    group_sum(ar2, ar2r, as_.at[2], ar_.at[2], my_y, 8, y_peer)
    edge12.wait()
    short_back(1)
    ar2s[...] = group_wait(ar2r, ar_.at[2])
    group_sum(ar2s, ar2q, as_.at[3], ar_.at[3], my_zc, 8, zc_peer)
    short_back(2)

    arrived(X_DH)

    def filt_block(b, _):
        R = pl.ds(pl.multiple_of(b * 128, 128), 128)
        lg[:, lanes(b)] = rb[X_DH, R, :].astype(F32).T
        return _

    lax.fori_loop(0, NB, filt_block, 0)
    stores.append(pltpu.make_async_copy(lg, lg_hbm, out_sem.at[4]))
    stores[4].start()

    a1 = group_wait(ar1q, ar_.at[1])
    gg[...] = a1[0:8]
    sg[0] = a1[8:8 + KS, 0:NG]
    a2 = group_wait(ar2q, ar_.at[3])
    sg[1] = a2[0:KS, 0:NG]
    sg[2] = a2[0:KS, NG:]

    for c in stores:
        c.wait()
    for k in range(6):
        sent(k)
    group_sent(nrb, ns, NH)
    group_sent(ar1r, as_.at[0], 8)
    group_sent(ar1q, as_.at[1], 8)
    group_sent(ar2r, as_.at[2], 8)
    group_sent(ar2q, as_.at[3], 8)


def hand_over(*refs):
    ins, outs, bufs, sem = refs[:5], refs[5:10], refs[10:15], refs[15]
    first = [pltpu.make_async_copy(a, b, sem.at[i]) for i, (a, b) in enumerate(zip(ins, bufs))]
    last = [pltpu.make_async_copy(b, c, sem.at[5 + i]) for i, (b, c) in enumerate(zip(bufs, outs))]
    for c in first:
        c.start()
    for a, c in zip(first, last):
        a.wait()
        c.start()
    for c in last:
        c.wait()


def on_device(projections, grouped_short_filters, long_filter, norm_gain, out_grad):
    anywhere = pl.BlockSpec(memory_space=pl.ANY)
    vmem = pl.BlockSpec(memory_space=pltpu.VMEM)
    tabs = tables()
    dma = pltpu.SemaphoreType.DMA
    res = pl.pallas_call(
        kernel,
        out_shape=[
            jax.ShapeDtypeStruct((NT, NC), BF16),
            jax.ShapeDtypeStruct((3, NT, NC), BF16),
            jax.ShapeDtypeStruct((3, KS, NG), F32),
            jax.ShapeDtypeStruct((NT, NC), F32),
            jax.ShapeDtypeStruct((8, 128), F32),
        ],
        in_specs=[anywhere, vmem, anywhere, vmem, anywhere] + [anywhere] * 8,
        out_specs=[anywhere, anywhere, vmem, anywhere, vmem],
        scratch_shapes=[
            pltpu.VMEM((NT, NC), BF16),
            pltpu.VMEM((3, NT, NC), BF16),
            pltpu.VMEM((NT, NC), F32),
            dma((5,)),
            pltpu.VMEM((3, NT, NC), BF16),
            pltpu.VMEM((NT, NC), F32),
            pltpu.VMEM((NT, NC), BF16),
            *[pltpu.VMEM(t.shape, t.dtype) for t in tabs],
            pltpu.VMEM((3, 16, NC), BF16),
            pltpu.VMEM((3, NT + 8, NC), F32),
            pltpu.VMEM((3, NT + 8, NC), F32),
            pltpu.VMEM((NT, NC), F32),
            pltpu.VMEM((NT, NC), F32),
            pltpu.VMEM((NC, NT), F32),
            pltpu.VMEM((NC, NT), F32),
            pltpu.VMEM((NC, NT), F32),
            pltpu.VMEM((3, 8, NC), F32),
            pltpu.VMEM((3, 8, NC), F32),
            pltpu.VMEM((6, NC, NT), BF16),
            pltpu.VMEM((6, NC, NT), BF16),
            pltpu.VMEM((NC, NT), F32),
            pltpu.VMEM((NC, 2 * NT), BF16),
            pltpu.VMEM((NC, 2 * NT), BF16),
            *[pltpu.VMEM((NC, 2 * NT), F32)] * 4,
            pltpu.VMEM((8, 128), F32),
            pltpu.VMEM((NH, 8, 128), F32),
            pltpu.VMEM((16, 128), F32),
            pltpu.VMEM((8, 16, 128), F32),
            pltpu.VMEM((16, 128), F32),
            pltpu.VMEM((8, 16, 128), F32),
            pltpu.VMEM((8, 128), F32),
            pltpu.VMEM((8, 8, 128), F32),
            pltpu.VMEM((8, 128), F32),
            pltpu.VMEM((8, 8, 128), F32),
            dma((11,)), dma((6,)), dma((6,)), dma((3,)), dma((3,)), dma, dma, dma((4,)), dma((4,)),
        ],
        compiler_params=pltpu.CompilerParams(
            collective_id=0, has_side_effects=True, vmem_limit_bytes=56 * 2**20),
    )(projections, grouped_short_filters, long_filter, norm_gain.reshape(8, 128), out_grad,
      *[jnp.asarray(t) for t in tabs])
    out, pg, sg, lg, gg = pl.pallas_call(
        hand_over,
        out_shape=[jax.ShapeDtypeStruct(r.shape, r.dtype) for r in res],
        in_specs=[anywhere] * 5,
        out_specs=[anywhere] * 5,
        scratch_shapes=[*[pltpu.VMEM(r.shape, r.dtype) for r in res], dma((10,))],
    )(*res)
    return out, pg, sg, lg, gg.reshape(NC)


def solution(mesh):
    in_specs = (P(None, "ctx", "ch"), P(None, None, "ch"), P("ctx", "ch"), P("ch"), P("ctx", "ch"))
    out_specs = (P("ctx", "ch"), P(None, "ctx", "ch"), P(None, None, "ch"), P("ctx", "ch"), P("ch"))
    return jax.shard_map(
        on_device, mesh=mesh, in_specs=in_specs, out_specs=out_specs, check_vma=False
    )
```
